32 devices in a mesh: grp: 2 (over y), gx: 16 (over z, x, core).
Axes of the slice: x: 2, y: 2, z: 4, core: 2. Of those that a mesh axis runs over, the one named last changes fastest.
Arguments:
- fields: float32 [32, 32, 256, 256], P('grp', 'gx'), parts along dimension 0, may hold values from -400 to 400
- factor_x: float32 [64, 96], P('grp'), parts along dimension 0, may hold values from -1 to 1
- factor_y: float32 [512, 96], P('grp'), parts along dimension 0, may hold values from -0.375 to 0.375
- factor_z: float32 [512, 96], P('grp'), parts along dimension 0, may hold values from -0.375 to 0.375
- factor_var: float32 [32, 8], P('grp'), parts along dimension 0, may hold values from -1.5 to 1.5
Outputs:
- core_tensor: float32 [18432, 8, 96], P(('grp', 'gx')), parts along dimension 0
- gram_vars: float32 [32, 16], P('grp'), parts along dimension 0
- gram_y: float32 [512, 256], P('grp'), parts along dimension 0
- gram_z: float32 [512, 256], P('grp'), parts along dimension 0
The draws below stay inside these ranges and needn't reach their ends.
There are 2 independent parts, one for each index of `grp`. The reference program is written for one: setup_inputs(seed, part) draws one part's arguments, and reference() takes and returns one part's arrays. A program takes and returns all parts, laid end to end along the dimension named above; each array names one. Nothing has to cross between parts.
All inputs are finite; a program needn't handle non-finite values.
Results may differ from the reference program's by a relative error of at most 0.000071.
Values sent between devices are 32-bit elements; how exact they have to be, the bound alone decides.
A program may use at most 64 MiB of HBM per device.

```python
import jax
import jax.numpy as jnp
from jax import lax

V = 16
R1 = 96
R2 = 96
R3 = 96
R4 = 8
N2 = 256
N3 = 256
N1 = 32


def draw_fields(key, part):
    key = jax.random.fold_in(key, 11)
    keys = jax.random.split(key, 5)
    low = jnp.log(0.3)
    high = jnp.log(3.0)
    scale_v = jnp.exp(jax.random.uniform(keys[1], (V, 1, 1, 1), jnp.float32, low, high))
    scale_y = jnp.exp(jax.random.uniform(keys[2], (1, 1, N2, 1), jnp.float32, low, high))
    scale_z = jnp.exp(jax.random.uniform(keys[3], (1, 1, 1, N3), jnp.float32, low, high))
    jitter = jnp.exp(jax.random.uniform(keys[4], (1, N1, 1, 1), jnp.float32, -0.3, 0.3))
    along = (jnp.arange(N1, dtype=jnp.float32) / float(max(N1 - 1, 1))).reshape(1, N1, 1, 1)
    trend = 3.0 ** (along - 0.5)
    base = jnp.clip(jax.random.normal(keys[0], (V, N1, N2, N3), jnp.float32), -4.0, 4.0)
    return (base * scale_v * scale_y * scale_z * trend * jitter).astype(jnp.float32)


def centred(stream_key, dims, width, most, kind=jnp.bfloat16):
    array = jax.random.normal(stream_key, dims, jnp.float32) * width
    return jnp.minimum(jnp.maximum(array, -most), most).astype(kind)


def setup_inputs(seed: int = 0, part: int = 0) -> dict:
    streams_of = jax.random.split(jax.random.key(seed), 6)
    part_keys = jax.random.split(jax.random.fold_in(streams_of[5], part), 6)
    return {
        "fields": draw_fields(jax.random.fold_in(jax.random.fold_in(streams_of[5], part), 71), part),
        "factor_x": centred(part_keys[1], (N1, R1), N1 ** -0.5, 1.0, jnp.float32),
        "factor_y": centred(part_keys[2], (N2, R2), N2 ** -0.5, 0.375, jnp.float32),
        "factor_z": centred(part_keys[3], (N3, R3), N3 ** -0.5, 0.375, jnp.float32),
        "factor_var": centred(part_keys[4], (V, R4), V ** -0.5, 1.5, jnp.float32),
    }


def reference(fields, factor_x, factor_y, factor_z, factor_var):
    highest = lax.Precision.HIGHEST
    reduced_var = jnp.einsum('va,vxyz->axyz', factor_var, fields, precision=highest)
    reduced_z = jnp.einsum('axyz,zk->axyk', reduced_var, factor_z, precision=highest)
    reduced_y = jnp.einsum('axyk,yj->xajk', reduced_z, factor_y, precision=highest)
    core_full = jnp.einsum('xajk,xr->jkar', reduced_y, factor_x, precision=highest)
    core_tensor = core_full.reshape(R2 * R3, R4, R1)
    gram_vars = jnp.einsum('vxyz,wxyz->vw', fields, fields, precision=highest) / float(N1 * N2 * N3)
    gram_y = jnp.einsum('vxyz,vxuz->yu', fields, fields, precision=highest) / float(V * N1 * N3)
    flat = fields.reshape(V * N1 * N2, N3)
    gram_z = jnp.dot(flat.T, flat, precision=highest, preferred_element_type=jnp.float32) / float(V * N1 * N2)
    return core_tensor, gram_vars, gram_y, gram_z
```

```python
import jax
import jax.numpy as jnp
from jax import lax
from jax.experimental import pallas as pl
from jax.experimental.pallas import tpu as pltpu
from jax.sharding import PartitionSpec as P

F32 = jnp.float32
BF16 = jnp.bfloat16
MESH = pl.DeviceIdType.MESH


def plain(fields, factor_x, factor_y, factor_z, factor_var):
    highest = lax.Precision.HIGHEST
    devices = lax.axis_size("gx")
    slab_rows = fields.shape[1]
    total_x = slab_rows * devices
    var_count = fields.shape[0]
    cells_y = fields.shape[2]
    cells_z = fields.shape[3]
    local_vars = jnp.einsum("vxyz,wxyz->vw", fields, fields, precision=highest)
    local_y = jnp.einsum("vxyz,vxuz->yu", fields, fields, precision=highest)
    flat = fields.reshape(-1, cells_z)
    local_z = jnp.dot(flat.T, flat, precision=highest, preferred_element_type=jnp.float32)
    summed_vars, summed_y, summed_z = lax.psum((local_vars, local_y, local_z), "gx")
    gram_vars = summed_vars / float(total_x * cells_y * cells_z)
    gram_y = summed_y / float(var_count * total_x * cells_z)
    gram_z = summed_z / float(var_count * total_x * cells_y)
    reduced_var = jnp.einsum("va,vxyz->axyz", factor_var, fields, precision=highest)
    reduced_z = jnp.einsum("axyz,zk->axyk", reduced_var, factor_z, precision=highest)
    reduced_y = jnp.einsum("axyk,yj->xajk", reduced_z, factor_y, precision=highest)
    comp_count = reduced_y.shape[1]
    projected = reduced_y.reshape(slab_rows, comp_count, reduced_y.shape[2] * reduced_y.shape[3])
    core_tensor = jnp.einsum(
        "xak,xr->kar",
        lax.all_to_all(projected, "gx", split_axis=2, concat_axis=0, tiled=True),
        factor_x,
        precision=highest,
    )
    return (core_tensor, gram_vars, gram_y, gram_z)


N = 16
V = 16
A = 8
S = 2
C = 256
R = 96
KP = 128
JD = R // N
CH = JD * S * A
GROUP = 4


def split(value):
    high = value.astype(BF16)
    return high, (value - high.astype(F32)).astype(BF16)


def dot(a, b):
    return jnp.dot(a, b, preferred_element_type=F32)


def kernel(f_ref, fx_ref, fy_ref, fz_ref, fv_ref, core_ref, gv_out, gy_out, gz_out,
           h_ref, l_ref, zhl, yhl, pad, w_ref, p_ref, r_ref, gy_acc, gz_acc, gv_acc,
           gram, half, quarter, eighth, recv_a, recv_b, recv_c, gv_all,
           s_core, r_core, s_gv, r_gv, s_a, r_a, s_b, r_b, s_c, r_c,
           s_cg, r_cg, s_bg, r_bg, s_ag, r_ag):
    me = lax.axis_index("gx")

    barrier = pltpu.get_barrier_semaphore()
    for off in range(1, N):
        pl.semaphore_signal(barrier, inc=1, device_id={"gx": lax.rem(me + off, N)}, device_id_type=MESH)

    def remote(src, dst, ssem, rsem, peer):
        return pltpu.make_async_remote_copy(
            src_ref=src, dst_ref=dst, send_sem=ssem, recv_sem=rsem,
            device_id={"gx": peer}, device_id_type=MESH)

    pad[...] = jnp.zeros((C, KP), F32)
    pad[:, 0:R] = fz_ref[...]
    z_high, z_low = split(pad[...])
    zhl[:, 0:KP] = z_high
    zhl[:, KP:2 * KP] = z_low
    pad[:, 0:R] = fy_ref[...]
    y_high, y_low = split(pad[...].T[0:R, :])
    yhl[0:R, :] = y_high
    yhl[R:2 * R, :] = y_low

    def project(i, carry):
        x = i // (V // GROUP)
        first = lax.rem(i, V // GROUP) * GROUP
        for u in range(GROUP):
            v = first + u
            high, low = split(f_ref[v, x])
            h_ref[v, x] = high
            l_ref[v, x] = low
            o = dot(yhl[...], jnp.concatenate([high, low], axis=1))
            along_y = o[0:R, 0:C] + (o[0:R, C:] + o[R:, 0:C])
            u_high, u_low = split(along_y)
            q = dot(jnp.concatenate([u_high, u_low], axis=0), zhl[...])
            w_ref[x * V + v] = q[0:R, 0:KP] + (q[0:R, KP:] + q[R:, 0:KP])
        return carry

    lax.fori_loop(0, S * V // GROUP, project, 0)

    for x in range(S):
        for a in range(A):
            total = fv_ref[0, a] * w_ref[x * V]
            for v in range(1, V):
                total = total + fv_ref[v, a] * w_ref[x * V + v]
            p_ref[pl.ds(x * A + a, R, stride=S * A), :] = total

    pl.semaphore_wait(barrier, N - 1)

    def chunk(index):
        return pl.ds(pl.multiple_of(index * CH, CH), CH)

    def core_copy(off):
        peer = lax.rem(me + off, N)
        return remote(p_ref.at[chunk(peer)], r_ref.at[chunk(me)], s_core.at[off], r_core.at[off], peer)

    for off in range(1, N):
        core_copy(off).start()
    r_ref[chunk(me), :] = p_ref[chunk(me), :]

    gy_acc[...] = jnp.zeros((2 * C, C), F32)
    gz_acc[...] = jnp.zeros((C, 2 * C), F32)
    gv_acc[...] = jnp.zeros((2 * C, C), F32)

    def grams(i, carry):
        x = i // (V // GROUP)
        first = lax.rem(i, V // GROUP) * GROUP
        highs = [h_ref[first + u, x] for u in range(GROUP)]
        lows = [l_ref[first + u, x] for u in range(GROUP)]
        turned = [h.T for h in highs]
        both = jnp.concatenate([jnp.concatenate(highs, axis=1), jnp.concatenate(lows, axis=1)], axis=0)
        gy_acc[...] += dot(both, jnp.concatenate(turned, axis=0))
        wide = jnp.concatenate([jnp.concatenate(highs, axis=0), jnp.concatenate(lows, axis=0)], axis=1)
        gz_acc[...] += dot(jnp.concatenate(turned, axis=1), wide)
        rows = [pl.ds(pl.multiple_of((first + u) * 16, 16), 16) for u in range(GROUP)]
        vh = jnp.concatenate([h_ref[:, x, r, :].reshape(C, C) for r in rows], axis=1)
        vl = jnp.concatenate([l_ref[:, x, r, :].reshape(C, C) for r in rows], axis=1)
        gv_acc[...] += lax.dot_general(
            jnp.concatenate([vh, vl], axis=0), vh, (((1,), (1,)), ((), ())), preferred_element_type=F32)
        return carry

    lax.fori_loop(0, S * V // GROUP, grams, 0)

    gram[0:C, :] = gy_acc[0:C, :] + (gy_acc[C:, :] + gy_acc[C:, :].T)
    gram[C:2 * C, :] = gz_acc[:, 0:C] + (gz_acc[:, C:] + gz_acc[:, C:].T)

    core = lax.rem(me, 2)
    xx = lax.rem(me // 2, 2)
    zz = me // 4
    pair = me + 1 - 2 * core
    xpair = me + 2 - 4 * xx

    def rows(start, size):
        return pl.ds(pl.multiple_of(start, size), size)

    copy_a = remote(gram.at[rows((1 - core) * C, C)], recv_a, s_a, r_a, pair)
    copy_a.start()

    row = lax.broadcasted_iota(jnp.int32, (C, C), 0)
    col = lax.broadcasted_iota(jnp.int32, (C, C), 1)
    whole = gv_acc[0:C, :] + (gv_acc[C:, :] + gv_acc[C:, :].T)
    kept = jnp.where(lax.rem(row, 16) == lax.rem(col, 16), whole, 0.0)
    pick_col = (lax.broadcasted_iota(jnp.int32, (C, KP), 0) // 16
                == lax.broadcasted_iota(jnp.int32, (C, KP), 1)).astype(F32)
    pick_row = (lax.broadcasted_iota(jnp.int32, (V, C), 1) // 16
                == lax.broadcasted_iota(jnp.int32, (V, C), 0)).astype(F32)
    highest = lax.Precision.HIGHEST
    by_col = jnp.dot(kept, pick_col, precision=highest, preferred_element_type=F32)
    gv_all[me] = jnp.dot(pick_row, by_col, precision=highest, preferred_element_type=F32)

    def gv_copy(off):
        return remote(gv_all.at[me], gv_all.at[me], s_gv.at[off], r_gv.at[off], lax.rem(me + off, N))

    for off in range(1, N):
        gv_copy(off).start()

    copy_a.wait()
    half[...] = gram[rows(core * C, C), :] + recv_a[...]
    copy_b = remote(half.at[rows((1 - xx) * 128, 128)], recv_b, s_b, r_b, xpair)
    copy_b.start()
    copy_b.wait()
    quarter[...] = half[rows(xx * 128, 128), :] + recv_b[...]

    def zpeer(off):
        return lax.rem(zz + off, 4)

    def c_copy(off):
        return remote(quarter.at[rows(zpeer(off) * 32, 32)], recv_c.at[off - 1],
                      s_c.at[off - 1], r_c.at[off - 1], zpeer(off) * 4 + lax.rem(me, 4))

    for off in range(1, 4):
        c_copy(off).start()
    for off in range(1, 4):
        c_copy(off).wait()
    mine = quarter[rows(zz * 32, 32), :] + (recv_c[0] + (recv_c[1] + recv_c[2]))
    scale = 1.0 / float(V * S * N * C)
    at = core * C + xx * 128 + zz * 32
    eighth[rows(at, 32), :] = mine * scale

    def cg_copy(off):
        return remote(eighth.at[rows(at, 32)], eighth.at[rows(at, 32)],
                      s_cg.at[off - 1], r_cg.at[off - 1], zpeer(off) * 4 + lax.rem(me, 4))

    for off in range(1, 4):
        cg_copy(off).start()
    for off in range(1, 4):
        cg_copy(off).wait()
    at_b = core * C + xx * 128
    copy_bg = remote(eighth.at[rows(at_b, 128)], eighth.at[rows(at_b, 128)], s_bg, r_bg, xpair)
    copy_bg.start()
    copy_bg.wait()
    at_a = core * C
    copy_ag = remote(eighth.at[rows(at_a, C)], eighth.at[rows(at_a, C)], s_ag, r_ag, pair)
    copy_ag.start()

    for off in range(1, N):
        core_copy(off).wait()
    fx_high, fx_low = split(jnp.concatenate(
        [fx_ref[pl.ds(x, N, stride=S), :] for x in range(S)], axis=0))
    weights = jnp.concatenate([fx_high, fx_high, fx_low], axis=0)
    for j in range(JD):
        for a in range(A):
            slab = jnp.concatenate(
                [r_ref[pl.ds(j * S * A + x * A + a, N, stride=CH), :] for x in range(S)], axis=0)
            high, low = split(slab)
            left = jnp.concatenate([high, low, high], axis=0)
            o = lax.dot_general(left, weights, (((0,), (0,)), ((), ())), preferred_element_type=F32)
            core_ref[pl.ds(j * R * A + a, R, stride=A), :] = o[0:R, :]

    for off in range(1, N):
        gv_copy(off).wait()
    total = gv_all[0]
    for d in range(1, N):
        total = total + gv_all[d]
    gv_out[...] = total[:, 0:V] * (1.0 / float(S * N * C * C))
    copy_ag.wait()
    gy_out[...] = eighth[0:C, :]
    gz_out[...] = eighth[C:2 * C, :]


def fused(fields, factor_x, factor_y, factor_z, factor_var):
    vmem = pl.BlockSpec(memory_space=pltpu.VMEM)
    dma = pltpu.SemaphoreType.DMA
    core, gv, gy, gz = pl.pallas_call(
        kernel,
        out_shape=(
            jax.ShapeDtypeStruct((JD * R * A, R), F32),
            jax.ShapeDtypeStruct((V, V), F32),
            jax.ShapeDtypeStruct((C, C), F32),
            jax.ShapeDtypeStruct((C, C), F32),
        ),
        in_specs=[vmem, vmem, vmem, vmem, pl.BlockSpec(memory_space=pltpu.SMEM)],
        out_specs=(vmem, vmem, vmem, vmem),
        scratch_shapes=[
            pltpu.VMEM((V, S, C, C), BF16), pltpu.VMEM((V, S, C, C), BF16),
            pltpu.VMEM((C, 2 * KP), BF16), pltpu.VMEM((2 * R, C), BF16), pltpu.VMEM((C, KP), F32),
            pltpu.VMEM((S * V, R, KP), F32),
            pltpu.VMEM((R * S * A, KP), F32), pltpu.VMEM((N * CH, KP), F32),
            pltpu.VMEM((2 * C, C), F32), pltpu.VMEM((C, 2 * C), F32), pltpu.VMEM((2 * C, C), F32),
            pltpu.VMEM((2 * C, C), F32), pltpu.VMEM((C, C), F32), pltpu.VMEM((128, C), F32),
            pltpu.VMEM((2 * C, C), F32),
            pltpu.VMEM((C, C), F32), pltpu.VMEM((128, C), F32), pltpu.VMEM((3, 32, C), F32),
            pltpu.VMEM((N, V, KP), F32),
            dma((N,)), dma((N,)), dma((N,)), dma((N,)),
            dma, dma, dma, dma, dma((3,)), dma((3,)),
            dma((3,)), dma((3,)), dma, dma, dma, dma,
        ],
        compiler_params=pltpu.CompilerParams(
            collective_id=0, has_side_effects=True, vmem_limit_bytes=56 * 1024 * 1024),
        name="fused",
    )(fields, factor_x, factor_y, factor_z, factor_var)
    return core.reshape(JD * R, A, R), gv, gy, gz


def local(fields, factor_x, factor_y, factor_z, factor_var):
    sizes = (fields.shape, factor_x.shape, factor_y.shape, factor_z.shape, factor_var.shape)
    served = ((V, S, C, C), (S * N, R), (C, R), (C, R), (V, A))
    if lax.axis_size("gx") == N and sizes == served:
        return fused(fields, factor_x, factor_y, factor_z, factor_var)
    return plain(fields, factor_x, factor_y, factor_z, factor_var)


def solution(mesh):
    in_specs = (
        P("grp", "gx", None, None),
        P("grp", None),
        P("grp", None),
        P("grp", None),
        P("grp", None),
    )
    out_specs = (P(("grp", "gx"), None, None), P("grp", None), P("grp", None), P("grp", None))
    return jax.shard_map(local, mesh=mesh, in_specs=in_specs, out_specs=out_specs, check_vma=False)
```

```python
import jax
import jax.numpy as jnp
from jax import lax
from jax.experimental import pallas as pl
from jax.experimental.pallas import tpu as pltpu
from jax.sharding import PartitionSpec as P

F32 = jnp.float32
BF16 = jnp.bfloat16
MESH = pl.DeviceIdType.MESH


def plain(fields, factor_x, factor_y, factor_z, factor_var):
    highest = lax.Precision.HIGHEST
    devices = lax.axis_size("gx")
    slab_rows = fields.shape[1]
    total_x = slab_rows * devices
    var_count = fields.shape[0]
    cells_y = fields.shape[2]
    cells_z = fields.shape[3]
    local_vars = jnp.einsum("vxyz,wxyz->vw", fields, fields, precision=highest)
    local_y = jnp.einsum("vxyz,vxuz->yu", fields, fields, precision=highest)
    flat = fields.reshape(-1, cells_z)
    local_z = jnp.dot(flat.T, flat, precision=highest, preferred_element_type=jnp.float32)
    summed_vars, summed_y, summed_z = lax.psum((local_vars, local_y, local_z), "gx")
    gram_vars = summed_vars / float(total_x * cells_y * cells_z)
    gram_y = summed_y / float(var_count * total_x * cells_z)
    gram_z = summed_z / float(var_count * total_x * cells_y)
    reduced_var = jnp.einsum("va,vxyz->axyz", factor_var, fields, precision=highest)
    reduced_z = jnp.einsum("axyz,zk->axyk", reduced_var, factor_z, precision=highest)
    reduced_y = jnp.einsum("axyk,yj->xajk", reduced_z, factor_y, precision=highest)
    comp_count = reduced_y.shape[1]
    projected = reduced_y.reshape(slab_rows, comp_count, reduced_y.shape[2] * reduced_y.shape[3])
    core_tensor = jnp.einsum(
        "xak,xr->kar",
        lax.all_to_all(projected, "gx", split_axis=2, concat_axis=0, tiled=True),
        factor_x,
        precision=highest,
    )
    return (core_tensor, gram_vars, gram_y, gram_z)


N = 16
V = 16
A = 8
S = 2
C = 256
R = 96
KP = 128
JD = R // N
CH = JD * S * A
GROUP = 4
TAIL = 24
PK = CH - TAIL
PIECE = 48


def split(value):
    high = value.astype(BF16)
    return high, (value - high.astype(F32)).astype(BF16)


def dot(a, b):
    return jnp.dot(a, b, preferred_element_type=F32)


def kernel(f_hbm, fy_ref, fz_ref, fv_ref, r_ref, gv_out, out,
           f_ref, h_ref, l_ref, zhl, yhl, pad, w_ref, p_ref, pk_ref, gy_acc, gz_acc, gv_acc,
           gram, recv_a, send_b, recv_b, send_c, recv_c, gv_all,
           s_load, s_core, r_core, s_gv, r_gv, s_a, r_a, s_b, r_b, s_c, r_c,
           s_cg, r_cg, s_bg, r_bg, s_ag, r_ag):
    me = lax.axis_index("gx")

    def load(i):
        x = i // (V // GROUP)
        first = lax.rem(i, V // GROUP) * GROUP
        part = pl.ds(first, GROUP)
        return pltpu.make_async_copy(f_hbm.at[part, x], f_ref.at[part, x], s_load.at[i])

    for i in range(S * V // GROUP):
        load(i).start()

    barrier = pltpu.get_barrier_semaphore()
    for off in range(1, N):
        pl.semaphore_signal(barrier, inc=1, device_id={"gx": lax.rem(me + off, N)}, device_id_type=MESH)

    def remote(src, dst, ssem, rsem, peer):
        return pltpu.make_async_remote_copy(
            src_ref=src, dst_ref=dst, send_sem=ssem, recv_sem=rsem,
            device_id={"gx": peer}, device_id_type=MESH)

    pad[...] = jnp.zeros((KP, C), F32)
    pad[0:R, :] = fz_ref[...]
    z_high, z_low = split(pad[...].T)
    zhl[:, 0:KP] = z_high
    zhl[:, KP:2 * KP] = z_low
    y_high, y_low = split(fy_ref[...])
    yhl[0:R, :] = y_high
    yhl[R:2 * R, :] = y_low

    def project(i, carry):
        x = i // (V // GROUP)
        first = lax.rem(i, V // GROUP) * GROUP
        load(i).wait()
        for u in range(GROUP):
            v = first + u
            high, low = split(f_ref[v, x])
            h_ref[v, x] = high
            l_ref[v, x] = low
            o = dot(yhl[...], jnp.concatenate([high, low], axis=1))
            along_y = o[0:R, 0:C] + (o[0:R, C:] + o[R:, 0:C])
            u_high, u_low = split(along_y)
            q = dot(jnp.concatenate([u_high, u_low], axis=0), zhl[...])
            w_ref[x * V + v] = q[0:R, 0:KP] + (q[0:R, KP:] + q[R:, 0:KP])
        return carry

    lax.fori_loop(0, S * V // GROUP, project, 0)

    for x in range(S):
        for a in range(A):
            total = fv_ref[a, 0] * w_ref[x * V]
            for v in range(1, V):
                total = total + fv_ref[a, v] * w_ref[x * V + v]
            p_ref[pl.ds(x * A + a, R, stride=S * A), :] = total

    lane = lax.broadcasted_iota(jnp.int32, (TAIL, KP), 1)
    for d in range(N):
        tail = p_ref[d * CH + PK:(d + 1) * CH, :]
        for t in range(3):
            rolled = pltpu.roll(tail, R - 32 * t, 1)
            pk_ref[d * PK + t * TAIL:d * PK + (t + 1) * TAIL, :] = jnp.where(
                lane >= R, rolled, p_ref[d * CH + t * TAIL:d * CH + (t + 1) * TAIL, :])

    pl.semaphore_wait(barrier, N - 1)

    q4 = lax.rem(me, 4)
    core = lax.rem(me, 2)
    xx = lax.rem(me // 2, 2)
    zz = me // 4
    pair = me + 1 - 2 * core
    xpair = me + 2 - 4 * xx

    def zpeer(off):
        return lax.rem(zz + off, 4)

    def chunk(index):
        return pl.ds(pl.multiple_of(index * PK, 8), PK)

    def core_copy(dz, dq):
        peer = zpeer(dz) * 4 + lax.rem(q4 + dq, 4)
        sem = dz * 4 + dq
        return remote(pk_ref.at[chunk(peer)], r_ref.at[chunk(me)], s_core.at[sem], r_core.at[sem], peer)

    others = [(dz, dq) for dz in (2, 1, 3, 0) for dq in range(4) if dz or dq]
    for dz, dq in others:
        core_copy(dz, dq).start()
    r_ref[chunk(me), :] = pk_ref[chunk(me), :]

    gy_acc[...] = jnp.zeros((2 * C, C), F32)
    gz_acc[...] = jnp.zeros((C, 2 * C), F32)
    gv_acc[...] = jnp.zeros((2 * C, C), F32)

    def grams(i, carry):
        x = i // (V // GROUP)
        first = lax.rem(i, V // GROUP) * GROUP
        highs = [h_ref[first + u, x] for u in range(GROUP)]
        lows = [l_ref[first + u, x] for u in range(GROUP)]
        turned = [h.T for h in highs]
        both = jnp.concatenate([jnp.concatenate(highs, axis=1), jnp.concatenate(lows, axis=1)], axis=0)
        gy_acc[...] += dot(both, jnp.concatenate(turned, axis=0))
        wide = jnp.concatenate([jnp.concatenate(highs, axis=0), jnp.concatenate(lows, axis=0)], axis=1)
        gz_acc[...] += dot(jnp.concatenate(turned, axis=1), wide)
        rows = [pl.ds(pl.multiple_of((first + u) * 16, 16), 16) for u in range(GROUP)]
        vh = jnp.concatenate([h_ref[:, x, r, :].reshape(C, C) for r in rows], axis=1)
        vl = jnp.concatenate([l_ref[:, x, r, :].reshape(C, C) for r in rows], axis=1)
        gv_acc[...] += lax.dot_general(
            jnp.concatenate([vh, vl], axis=0), vh, (((1,), (1,)), ((), ())), preferred_element_type=F32)
        return carry

    lax.fori_loop(0, S * V // GROUP, grams, 0)

    whole_y = gy_acc[0:C, :] + (gy_acc[C:, :] + gy_acc[C:, :].T)
    whole_z = gz_acc[:, 0:C] + (gz_acc[:, C:] + gz_acc[:, C:].T)
    for m, whole in enumerate((whole_y, whole_z)):
        gram[m * 384:m * 384 + 128, :] = whole[0:128, 0:128]
        gram[m * 384 + 128:m * 384 + 256, :] = whole[0:128, 128:]
        gram[m * 384 + 256:m * 384 + 384, :] = whole[128:, 128:]

    def piece(c, x, z):
        return pl.ds(pl.multiple_of(((c * 2 + x) * 4 + z) * PIECE, 8), PIECE)

    order = (1, 2, 3, 0)

    def a_copy(k, off):
        x = (1 - xx) if k == 0 else xx
        sem = k * 4 + off
        return remote(gram.at[piece(1 - core, x, zpeer(off))], recv_a.at[sem], s_a.at[sem], r_a.at[sem], pair)

    for k in range(2):
        for off in order:
            a_copy(k, off).start()

    row = lax.broadcasted_iota(jnp.int32, (C, C), 0)
    col = lax.broadcasted_iota(jnp.int32, (C, C), 1)
    whole = gv_acc[0:C, :] + (gv_acc[C:, :] + gv_acc[C:, :].T)
    kept = jnp.where(lax.rem(row, 16) == lax.rem(col, 16), whole, 0.0)
    pick_col = (lax.broadcasted_iota(jnp.int32, (C, KP), 0) // 16
                == lax.broadcasted_iota(jnp.int32, (C, KP), 1)).astype(F32)
    pick_row = (lax.broadcasted_iota(jnp.int32, (V, C), 1) // 16
                == lax.broadcasted_iota(jnp.int32, (V, C), 0)).astype(F32)
    highest = lax.Precision.HIGHEST
    by_col = jnp.dot(kept, pick_col, precision=highest, preferred_element_type=F32)
    by_both = jnp.dot(pick_row, by_col, precision=highest, preferred_element_type=F32)
    gv_all[me] = by_both[0:8, :] + pltpu.roll(by_both[8:16, :], 16, 1)

    def gv_copy(off):
        return remote(gv_all.at[me], gv_all.at[me], s_gv.at[off], r_gv.at[off], lax.rem(me + off, N))

    def b_copy(off):
        return remote(send_b.at[off], recv_b.at[off], s_b.at[off], r_b.at[off], xpair)

    def c_copy(off):
        return remote(send_c.at[off], recv_c.at[off], s_c.at[off], r_c.at[off], zpeer(off) * 4 + q4)

    for off in order:
        a_copy(0, off).wait()
        send_b[off] = gram[piece(core, 1 - xx, zpeer(off)), :] + recv_a[off]
        b_copy(off).start()
    for off in order:
        a_copy(1, off).wait()
        partial = gram[piece(core, xx, zpeer(off)), :] + recv_a[4 + off]
        b_copy(off).wait()
        send_c[off] = partial + recv_b[off]
        if off:
            c_copy(off).start()
    for off in range(1, N):
        gv_copy(off).start()
    mine = send_c[0]
    for off in range(1, 4):
        c_copy(off).wait()
        mine = mine + recv_c[off]
    out[piece(core, xx, zz), :] = mine * (1.0 / float(V * S * N * C))

    def cg_copy(off):
        at = piece(core, xx, zz)
        return remote(out.at[at], out.at[at], s_cg.at[off], r_cg.at[off], zpeer(off) * 4 + q4)

    def bg_copy(off):
        at = piece(core, xx, zpeer(4 - off))
        return remote(out.at[at], out.at[at], s_bg.at[off], r_bg.at[off], xpair)

    def ag_copy(k, off):
        at = piece(core, xx if k == 0 else 1 - xx, zpeer(4 - off))
        sem = k * 4 + off
        return remote(out.at[at], out.at[at], s_ag.at[sem], r_ag.at[sem], pair)

    for off in range(1, 4):
        cg_copy(off).start()
    for off in range(4):
        if off:
            cg_copy(off).wait()
        bg_copy(off).start()
        ag_copy(0, off).start()
    for off in range(4):
        bg_copy(off).wait()
        ag_copy(1, off).start()

    for off in range(1, N):
        gv_copy(off).wait()
    total = gv_all[0]
    for d in range(1, N):
        total = total + gv_all[d]
    gv_out[...] = total
    for dz, dq in others:
        core_copy(dz, dq).wait()
    for k in range(2):
        for off in range(4):
            ag_copy(k, off).wait()


def finish(r_ref, fx_ref, gram_ref, gv_ref, core_hbm, gv_out, gy_out, gz_out, un_ref, core_ref, sems):
    lane = lax.broadcasted_iota(jnp.int32, (TAIL, KP), 1)
    for d in range(N):
        parts = [r_ref[d * PK + t * TAIL:d * PK + (t + 1) * TAIL, :] for t in range(3)]
        for t in range(3):
            un_ref[d * CH + t * TAIL:d * CH + (t + 1) * TAIL, :] = parts[t]
        rolled = [pltpu.roll(parts[t], 32 * (t + 1), 1) for t in range(3)]
        un_ref[d * CH + PK:(d + 1) * CH, :] = jnp.where(
            lane < 32, rolled[0], jnp.where(lane < 64, rolled[1], rolled[2]))

    fx_high, fx_low = split(jnp.concatenate(
        [fx_ref[pl.ds(x, N, stride=S), :] for x in range(S)], axis=0))
    weights = jnp.concatenate([fx_high, fx_high, fx_low], axis=0).T
    copies = []
    for a in range(A):
        slabs = [jnp.concatenate(
            [un_ref[pl.ds(j * S * A + x * A + a, N, stride=CH), 0:R] for x in range(S)], axis=0)
            for j in range(JD)]
        high, low = split(jnp.concatenate(slabs, axis=1))
        core_ref[a] = dot(weights, jnp.concatenate([high, low, high], axis=0))
        copy = pltpu.make_async_copy(core_ref.at[a], core_hbm.at[a], sems.at[a])
        copy.start()
        copies.append(copy)

    scale = 1.0 / float(S * N * C * C)
    gv_out[0:8, :] = gv_ref[:, 0:V] * scale
    gv_out[8:16, :] = gv_ref[:, V:2 * V] * scale
    for m, o_ref in enumerate((gy_out, gz_out)):
        o_ref[0:128, 0:128] = gram_ref[m * 384:m * 384 + 128, :]
        off_block = gram_ref[m * 384 + 128:m * 384 + 256, :]
        o_ref[0:128, 128:] = off_block
        o_ref[128:, 0:128] = off_block.T
        o_ref[128:, 128:] = gram_ref[m * 384 + 256:m * 384 + 384, :]
    for copy in copies:
        copy.wait()


def fused(fields, factor_x, factor_y, factor_z, factor_var):
    vmem = pl.BlockSpec(memory_space=pltpu.VMEM)
    anywhere = pl.BlockSpec(memory_space=pl.ANY)
    dma = pltpu.SemaphoreType.DMA
    received, gv, gram = pl.pallas_call(
        kernel,
        out_shape=(
            jax.ShapeDtypeStruct((N * PK, KP), F32),
            jax.ShapeDtypeStruct((8, KP), F32),
            jax.ShapeDtypeStruct((16 * PIECE, 128), F32),
        ),
        in_specs=[anywhere, vmem, vmem, pl.BlockSpec(memory_space=pltpu.SMEM)],
        out_specs=(vmem, vmem, vmem),
        scratch_shapes=[
            pltpu.VMEM((V, S, C, C), F32),
            pltpu.VMEM((V, S, C, C), BF16), pltpu.VMEM((V, S, C, C), BF16),
            pltpu.VMEM((C, 2 * KP), BF16), pltpu.VMEM((2 * R, C), BF16), pltpu.VMEM((KP, C), F32),
            pltpu.VMEM((S * V, R, KP), F32),
            pltpu.VMEM((R * S * A, KP), F32), pltpu.VMEM((N * PK, KP), F32),
            pltpu.VMEM((2 * C, C), F32), pltpu.VMEM((C, 2 * C), F32), pltpu.VMEM((2 * C, C), F32),
            pltpu.VMEM((16 * PIECE, 128), F32), pltpu.VMEM((8, PIECE, 128), F32),
            pltpu.VMEM((4, PIECE, 128), F32), pltpu.VMEM((4, PIECE, 128), F32),
            pltpu.VMEM((4, PIECE, 128), F32), pltpu.VMEM((4, PIECE, 128), F32),
            pltpu.VMEM((N, 8, KP), F32),
            dma((S * V // GROUP,)), dma((N,)), dma((N,)), dma((N,)), dma((N,)),
            dma((8,)), dma((8,)), dma((4,)), dma((4,)), dma((4,)), dma((4,)),
            dma((4,)), dma((4,)), dma((4,)), dma((4,)), dma((8,)), dma((8,)),
        ],
        compiler_params=pltpu.CompilerParams(
            collective_id=0, has_side_effects=True, vmem_limit_bytes=56 * 1024 * 1024),
        name="fused",
    )(fields, factor_y.T, factor_z.T, factor_var.T)
    core, gram_v, gram_y, gram_z = pl.pallas_call(
        finish,
        out_shape=(
            jax.ShapeDtypeStruct((A, R, JD * R), F32),
            jax.ShapeDtypeStruct((V, V), F32),
            jax.ShapeDtypeStruct((C, C), F32),
            jax.ShapeDtypeStruct((C, C), F32),
        ),
        in_specs=[vmem] * 4,
        out_specs=(anywhere, vmem, vmem, vmem),
        scratch_shapes=[pltpu.VMEM((N * CH, KP), F32), pltpu.VMEM((A, R, JD * R), F32), dma((A,))],
        compiler_params=pltpu.CompilerParams(vmem_limit_bytes=32 * 1024 * 1024),
        name="finish",
    )(received, factor_x, gram, gv)
    return core.transpose(2, 0, 1), gram_v, gram_y, gram_z


def local(fields, factor_x, factor_y, factor_z, factor_var):
    sizes = (fields.shape, factor_x.shape, factor_y.shape, factor_z.shape, factor_var.shape)
    served = ((V, S, C, C), (S * N, R), (C, R), (C, R), (V, A))
    if lax.axis_size("gx") == N and sizes == served:
        return fused(fields, factor_x, factor_y, factor_z, factor_var)
    return plain(fields, factor_x, factor_y, factor_z, factor_var)


def solution(mesh):
    in_specs = (
        P("grp", "gx", None, None),
        P("grp", None),
        P("grp", None),
        P("grp", None),
        P("grp", None),
    )
    out_specs = (P(("grp", "gx"), None, None), P("grp", None), P("grp", None), P("grp", None))
    return jax.shard_map(local, mesh=mesh, in_specs=in_specs, out_specs=out_specs, check_vma=False)
```

```python
import jax
import jax.numpy as jnp
from jax import lax
from jax.experimental import pallas as pl
from jax.experimental.pallas import tpu as pltpu
from jax.sharding import PartitionSpec as P

F32 = jnp.float32
BF16 = jnp.bfloat16
MESH = pl.DeviceIdType.MESH


def plain(fields, factor_x, factor_y, factor_z, factor_var):
    highest = lax.Precision.HIGHEST
    devices = lax.axis_size("gx")
    slab_rows = fields.shape[1]
    total_x = slab_rows * devices
    var_count = fields.shape[0]
    cells_y = fields.shape[2]
    cells_z = fields.shape[3]
    local_vars = jnp.einsum("vxyz,wxyz->vw", fields, fields, precision=highest)
    local_y = jnp.einsum("vxyz,vxuz->yu", fields, fields, precision=highest)
    flat = fields.reshape(-1, cells_z)
    local_z = jnp.dot(flat.T, flat, precision=highest, preferred_element_type=jnp.float32)
    summed_vars, summed_y, summed_z = lax.psum((local_vars, local_y, local_z), "gx")
    gram_vars = summed_vars / float(total_x * cells_y * cells_z)
    gram_y = summed_y / float(var_count * total_x * cells_z)
    gram_z = summed_z / float(var_count * total_x * cells_y)
    reduced_var = jnp.einsum("va,vxyz->axyz", factor_var, fields, precision=highest)
    reduced_z = jnp.einsum("axyz,zk->axyk", reduced_var, factor_z, precision=highest)
    reduced_y = jnp.einsum("axyk,yj->xajk", reduced_z, factor_y, precision=highest)
    comp_count = reduced_y.shape[1]
    projected = reduced_y.reshape(slab_rows, comp_count, reduced_y.shape[2] * reduced_y.shape[3])
    core_tensor = jnp.einsum(
        "xak,xr->kar",
        lax.all_to_all(projected, "gx", split_axis=2, concat_axis=0, tiled=True),
        factor_x,
        precision=highest,
    )
    return (core_tensor, gram_vars, gram_y, gram_z)


N = 16
V = 16
A = 8
S = 2
C = 256
R = 96
KP = 128
JD = R // N
CH = JD * S * A
GROUP = 4
TAIL = 24
PK = CH - TAIL
PIECE = 48


def split(value):
    high = value.astype(BF16)
    return high, (value - high.astype(F32)).astype(BF16)


def dot(a, b):
    return jnp.dot(a, b, preferred_element_type=F32)


def kernel(f_hbm, fy_ref, fz_ref, fv_ref, r_ref, gv_out, out,
           f_ref, h_ref, l_ref, zhl, yhl, pad, w_ref, p_ref, pk_ref, gy_acc, gz_acc, gv_acc,
           gram, recv_a, send_b, recv_b, send_c, recv_c, gv_all,
           s_load, s_core, r_core, s_gv, r_gv, s_a, r_a, s_b, r_b, s_c, r_c,
           s_cg, r_cg, s_bg, r_bg, s_ag, r_ag):
    me = lax.axis_index("gx")

    def load(i):
        x = i // (V // GROUP)
        first = lax.rem(i, V // GROUP) * GROUP
        part = pl.ds(first, GROUP)
        return pltpu.make_async_copy(f_hbm.at[part, x], f_ref.at[part, x], s_load.at[i])

    for i in range(S * V // GROUP):
        load(i).start()

    barrier = pltpu.get_barrier_semaphore()
    for off in range(1, N):
        pl.semaphore_signal(barrier, inc=1, device_id={"gx": lax.rem(me + off, N)}, device_id_type=MESH)

    def remote(src, dst, ssem, rsem, peer):
        return pltpu.make_async_remote_copy(
            src_ref=src, dst_ref=dst, send_sem=ssem, recv_sem=rsem,
            device_id={"gx": peer}, device_id_type=MESH)

    pad[...] = jnp.zeros((KP, C), F32)
    pad[0:R, :] = fz_ref[...]
    z_high, z_low = split(pad[...].T)
    zhl[:, 0:KP] = z_high
    zhl[:, KP:2 * KP] = z_low
    y_high, y_low = split(fy_ref[...])
    yhl[0:R, :] = y_high
    yhl[R:2 * R, :] = y_low

    def project(i, carry):
        x = i // (V // GROUP)
        first = lax.rem(i, V // GROUP) * GROUP
        load(i).wait()
        for u in range(GROUP):
            v = first + u
            high, low = split(f_ref[v, x])
            h_ref[v, x] = high
            l_ref[v, x] = low
            o = dot(yhl[...], jnp.concatenate([high, low], axis=1))
            along_y = o[0:R, 0:C] + (o[0:R, C:] + o[R:, 0:C])
            u_high, u_low = split(along_y)
            q = dot(jnp.concatenate([u_high, u_low], axis=0), zhl[...])
            w_ref[x * V + v] = q[0:R, 0:KP] + (q[0:R, KP:] + q[R:, 0:KP])
        return carry

    lax.fori_loop(0, S * V // GROUP, project, 0)

    for x in range(S):
        for a in range(A):
            total = fv_ref[a, 0] * w_ref[x * V]
            for v in range(1, V):
                total = total + fv_ref[a, v] * w_ref[x * V + v]
            p_ref[pl.ds(x * A + a, R, stride=S * A), :] = total

    lane = lax.broadcasted_iota(jnp.int32, (TAIL, KP), 1)
    for d in range(N):
        tail = p_ref[d * CH + PK:(d + 1) * CH, :]
        for t in range(3):
            rolled = pltpu.roll(tail, R - 32 * t, 1)
            pk_ref[d * PK + t * TAIL:d * PK + (t + 1) * TAIL, :] = jnp.where(
                lane >= R, rolled, p_ref[d * CH + t * TAIL:d * CH + (t + 1) * TAIL, :])

    pl.semaphore_wait(barrier, N - 1)

    q4 = lax.rem(me, 4)
    core = lax.rem(me, 2)
    xx = lax.rem(me // 2, 2)
    zz = me // 4
    pair = me + 1 - 2 * core
    xpair = me + 2 - 4 * xx

    def zpeer(off):
        return lax.rem(zz + off, 4)

    def chunk(index):
        return pl.ds(pl.multiple_of(index * PK, 8), PK)

    def core_copy(dz, dq):
        peer = zpeer(dz) * 4 + lax.rem(q4 + dq, 4)
        sem = dz * 4 + dq
        return remote(pk_ref.at[chunk(peer)], r_ref.at[chunk(me)], s_core.at[sem], r_core.at[sem], peer)

    others = [(dz, dq) for dz in (2, 1, 3, 0) for dq in range(4) if dz or dq]
    for dz, dq in others:
        core_copy(dz, dq).start()
    r_ref[chunk(me), :] = pk_ref[chunk(me), :]

    gy_acc[...] = jnp.zeros((2 * C, C), F32)
    gz_acc[...] = jnp.zeros((C, 2 * C), F32)
    gv_acc[...] = jnp.zeros((2 * C, C), F32)

    def grams(i, carry):
        x = i // (V // GROUP)
        first = lax.rem(i, V // GROUP) * GROUP
        highs = [h_ref[first + u, x] for u in range(GROUP)]
        lows = [l_ref[first + u, x] for u in range(GROUP)]
        turned = [h.T for h in highs]
        both = jnp.concatenate([jnp.concatenate(highs, axis=1), jnp.concatenate(lows, axis=1)], axis=0)
        gy_acc[...] += dot(both, jnp.concatenate(turned, axis=0))
        wide = jnp.concatenate([jnp.concatenate(highs, axis=0), jnp.concatenate(lows, axis=0)], axis=1)
        gz_acc[...] += dot(jnp.concatenate(turned, axis=1), wide)
        return carry

    lax.fori_loop(0, S * V // GROUP, grams, 0)

    def gram_v(i, carry):
        x = i // (V // GROUP)
        first = lax.rem(i, V // GROUP) * GROUP
        rows = [pl.ds(pl.multiple_of((first + u) * 16, 16), 16) for u in range(GROUP)]
        vh = jnp.concatenate([h_ref[:, x, r, :].reshape(C, C) for r in rows], axis=1)
        vl = jnp.concatenate([l_ref[:, x, r, :].reshape(C, C) for r in rows], axis=1)
        gv_acc[...] += lax.dot_general(
            jnp.concatenate([vh, vl], axis=0), vh, (((1,), (1,)), ((), ())), preferred_element_type=F32)
        return carry

    whole_y = gy_acc[0:C, :] + (gy_acc[C:, :] + gy_acc[C:, :].T)
    whole_z = gz_acc[:, 0:C] + (gz_acc[:, C:] + gz_acc[:, C:].T)
    for m, whole in enumerate((whole_y, whole_z)):
        gram[m * 384:m * 384 + 128, :] = whole[0:128, 0:128]
        gram[m * 384 + 128:m * 384 + 256, :] = whole[0:128, 128:]
        gram[m * 384 + 256:m * 384 + 384, :] = whole[128:, 128:]

    def piece(c, x, z):
        return pl.ds(pl.multiple_of(((c * 2 + x) * 4 + z) * PIECE, 8), PIECE)

    order = (1, 2, 3, 0)

    def a_copy(k, off):
        x = (1 - xx) if k == 0 else xx
        sem = k * 4 + off
        return remote(gram.at[piece(1 - core, x, zpeer(off))], recv_a.at[sem], s_a.at[sem], r_a.at[sem], pair)

    for k in range(2):
        for off in order:
            a_copy(k, off).start()

    lax.fori_loop(0, V // GROUP, gram_v, 0)

    def gv_copy(off):
        return remote(gv_all.at[me], gv_all.at[me], s_gv.at[off], r_gv.at[off], lax.rem(me + off, N))

    def b_copy(off):
        return remote(send_b.at[off], recv_b.at[off], s_b.at[off], r_b.at[off], xpair)

    def c_copy(off):
        return remote(send_c.at[off], recv_c.at[off], s_c.at[off], r_c.at[off], zpeer(off) * 4 + q4)

    for off in order:
        a_copy(0, off).wait()
        send_b[off] = gram[piece(core, 1 - xx, zpeer(off)), :] + recv_a[off]
        b_copy(off).start()

    lax.fori_loop(V // GROUP, S * V // GROUP, gram_v, 0)
    for off in order:
        a_copy(1, off).wait()
        partial = gram[piece(core, xx, zpeer(off)), :] + recv_a[4 + off]
        b_copy(off).wait()
        send_c[off] = partial + recv_b[off]
        if off:
            c_copy(off).start()
    row = lax.broadcasted_iota(jnp.int32, (C, C), 0)
    col = lax.broadcasted_iota(jnp.int32, (C, C), 1)
    whole = gv_acc[0:C, :] + (gv_acc[C:, :] + gv_acc[C:, :].T)
    kept = jnp.where(lax.rem(row, 16) == lax.rem(col, 16), whole, 0.0)
    pick_col = (lax.broadcasted_iota(jnp.int32, (C, KP), 0) // 16
                == lax.broadcasted_iota(jnp.int32, (C, KP), 1)).astype(F32)
    pick_row = (lax.broadcasted_iota(jnp.int32, (V, C), 1) // 16
                == lax.broadcasted_iota(jnp.int32, (V, C), 0)).astype(F32)
    highest = lax.Precision.HIGHEST
    by_col = jnp.dot(kept, pick_col, precision=highest, preferred_element_type=F32)
    by_both = jnp.dot(pick_row, by_col, precision=highest, preferred_element_type=F32)
    gv_all[me] = by_both[0:8, :] + pltpu.roll(by_both[8:16, :], 16, 1)

    for off in range(1, N):
        gv_copy(off).start()
    mine = send_c[0]
    for off in range(1, 4):
        c_copy(off).wait()
        mine = mine + recv_c[off]
    out[piece(core, xx, zz), :] = mine * (1.0 / float(V * S * N * C))

    def cg_copy(off):
        at = piece(core, xx, zz)
        return remote(out.at[at], out.at[at], s_cg.at[off], r_cg.at[off], zpeer(off) * 4 + q4)

    def bg_copy(off):
        at = piece(core, xx, zpeer(4 - off))
        return remote(out.at[at], out.at[at], s_bg.at[off], r_bg.at[off], xpair)

    def ag_copy(k, off):
        at = piece(core, xx if k == 0 else 1 - xx, zpeer(4 - off))
        sem = k * 4 + off
        return remote(out.at[at], out.at[at], s_ag.at[sem], r_ag.at[sem], pair)

    for off in range(1, 4):
        cg_copy(off).start()
    for off in range(4):
        if off:
            cg_copy(off).wait()
        bg_copy(off).start()
        ag_copy(0, off).start()
    for off in range(4):
        bg_copy(off).wait()
        ag_copy(1, off).start()

    for off in range(1, N):
        gv_copy(off).wait()
    total = gv_all[0]
    for d in range(1, N):
        total = total + gv_all[d]
    gv_out[...] = total
    for dz, dq in others:
        core_copy(dz, dq).wait()
    for k in range(2):
        for off in range(4):
            ag_copy(k, off).wait()


def finish(r_hbm, fx_ref, gram_hbm, gv_hbm, core_hbm, gv_out, gy_out, gz_out,
           r_ref, gram_ref, gv_ref, un_ref, core_ref, s_in, sems):
    loads = [pltpu.make_async_copy(src, dst, s_in.at[i]) for i, (src, dst) in enumerate(
        ((r_hbm, r_ref), (gram_hbm, gram_ref), (gv_hbm, gv_ref)))]
    for load in loads:
        load.start()
    loads[0].wait()

    lane = lax.broadcasted_iota(jnp.int32, (TAIL, KP), 1)
    for d in range(N):
        parts = [r_ref[d * PK + t * TAIL:d * PK + (t + 1) * TAIL, :] for t in range(3)]
        for t in range(3):
            un_ref[d * CH + t * TAIL:d * CH + (t + 1) * TAIL, :] = parts[t]
        rolled = [pltpu.roll(parts[t], 32 * (t + 1), 1) for t in range(3)]
        un_ref[d * CH + PK:(d + 1) * CH, :] = jnp.where(
            lane < 32, rolled[0], jnp.where(lane < 64, rolled[1], rolled[2]))

    fx_high, fx_low = split(jnp.concatenate(
        [fx_ref[pl.ds(x, N, stride=S), :] for x in range(S)], axis=0))
    weights = jnp.concatenate([fx_high, fx_high, fx_low], axis=0).T
    copies = []
    for a in range(A):
        slabs = [jnp.concatenate(
            [un_ref[pl.ds(j * S * A + x * A + a, N, stride=CH), 0:R] for x in range(S)], axis=0)
            for j in range(JD)]
        high, low = split(jnp.concatenate(slabs, axis=1))
        core_ref[a] = dot(weights, jnp.concatenate([high, low, high], axis=0))
        copy = pltpu.make_async_copy(core_ref.at[a], core_hbm.at[a], sems.at[a])
        copy.start()
        copies.append(copy)

    loads[1].wait()
    loads[2].wait()
    scale = 1.0 / float(S * N * C * C)
    gv_out[0:8, :] = gv_ref[:, 0:V] * scale
    gv_out[8:16, :] = gv_ref[:, V:2 * V] * scale
    for m, o_ref in enumerate((gy_out, gz_out)):
        o_ref[0:128, 0:128] = gram_ref[m * 384:m * 384 + 128, :]
        off_block = gram_ref[m * 384 + 128:m * 384 + 256, :]
        o_ref[0:128, 128:] = off_block
        o_ref[128:, 0:128] = off_block.T
        o_ref[128:, 128:] = gram_ref[m * 384 + 256:m * 384 + 384, :]
    for copy in copies:
        copy.wait()


def fused(fields, factor_x, factor_y, factor_z, factor_var):
    vmem = pl.BlockSpec(memory_space=pltpu.VMEM)
    anywhere = pl.BlockSpec(memory_space=pl.ANY)
    in_hbm = pl.BlockSpec(memory_space=pltpu.HBM)
    dma = pltpu.SemaphoreType.DMA
    received, gv, gram = pl.pallas_call(
        kernel,
        out_shape=(
            jax.ShapeDtypeStruct((N * PK, KP), F32),
            jax.ShapeDtypeStruct((8, KP), F32),
            jax.ShapeDtypeStruct((16 * PIECE, 128), F32),
        ),
        in_specs=[anywhere, vmem, vmem, pl.BlockSpec(memory_space=pltpu.SMEM)],
        out_specs=(vmem, vmem, vmem),
        scratch_shapes=[
            pltpu.VMEM((V, S, C, C), F32),
            pltpu.VMEM((V, S, C, C), BF16), pltpu.VMEM((V, S, C, C), BF16),
            pltpu.VMEM((C, 2 * KP), BF16), pltpu.VMEM((2 * R, C), BF16), pltpu.VMEM((KP, C), F32),
            pltpu.VMEM((S * V, R, KP), F32),
            pltpu.VMEM((R * S * A, KP), F32), pltpu.VMEM((N * PK, KP), F32),
            pltpu.VMEM((2 * C, C), F32), pltpu.VMEM((C, 2 * C), F32), pltpu.VMEM((2 * C, C), F32),
            pltpu.VMEM((16 * PIECE, 128), F32), pltpu.VMEM((8, PIECE, 128), F32),
            pltpu.VMEM((4, PIECE, 128), F32), pltpu.VMEM((4, PIECE, 128), F32),
            pltpu.VMEM((4, PIECE, 128), F32), pltpu.VMEM((4, PIECE, 128), F32),
            pltpu.VMEM((N, 8, KP), F32),
            dma((S * V // GROUP,)), dma((N,)), dma((N,)), dma((N,)), dma((N,)),
            dma((8,)), dma((8,)), dma((4,)), dma((4,)), dma((4,)), dma((4,)),
            dma((4,)), dma((4,)), dma((4,)), dma((4,)), dma((8,)), dma((8,)),
        ],
        compiler_params=pltpu.CompilerParams(
            collective_id=0, has_side_effects=True, vmem_limit_bytes=56 * 1024 * 1024),
        name="fused",
    )(fields, factor_y.T, factor_z.T, factor_var.T)
    core, gram_v, gram_y, gram_z = pl.pallas_call(
        finish,
        out_shape=(
            jax.ShapeDtypeStruct((A, R, JD * R), F32),
            jax.ShapeDtypeStruct((V, V), F32),
            jax.ShapeDtypeStruct((C, C), F32),
            jax.ShapeDtypeStruct((C, C), F32),
        ),
        in_specs=[in_hbm, vmem, in_hbm, in_hbm],
        out_specs=(anywhere, vmem, vmem, vmem),
        scratch_shapes=[
            pltpu.VMEM((N * PK, KP), F32), pltpu.VMEM((16 * PIECE, 128), F32), pltpu.VMEM((8, KP), F32),
            pltpu.VMEM((N * CH, KP), F32), pltpu.VMEM((A, R, JD * R), F32), dma((3,)), dma((A,))],
        compiler_params=pltpu.CompilerParams(vmem_limit_bytes=60 * 1024 * 1024),
        name="finish",
    )(received, factor_x, gram, gv)
    return core.transpose(2, 0, 1), gram_v, gram_y, gram_z


def local(fields, factor_x, factor_y, factor_z, factor_var):
    sizes = (fields.shape, factor_x.shape, factor_y.shape, factor_z.shape, factor_var.shape)
    served = ((V, S, C, C), (S * N, R), (C, R), (C, R), (V, A))
    if lax.axis_size("gx") == N and sizes == served:
        return fused(fields, factor_x, factor_y, factor_z, factor_var)
    return plain(fields, factor_x, factor_y, factor_z, factor_var)


def solution(mesh):
    in_specs = (
        P("grp", "gx", None, None),
        P("grp", None),
        P("grp", None),
        P("grp", None),
        P("grp", None),
    )
    out_specs = (P(("grp", "gx"), None, None), P("grp", None), P("grp", None), P("grp", None))
    return jax.shard_map(local, mesh=mesh, in_specs=in_specs, out_specs=out_specs, check_vma=False)
```

```python
import jax
import jax.numpy as jnp
from jax import lax
from jax.experimental import pallas as pl
from jax.experimental.pallas import tpu as pltpu
from jax.sharding import PartitionSpec as P

F32 = jnp.float32
BF16 = jnp.bfloat16
MESH = pl.DeviceIdType.MESH


def plain(fields, factor_x, factor_y, factor_z, factor_var):
    highest = lax.Precision.HIGHEST
    devices = lax.axis_size("gx")
    slab_rows = fields.shape[1]
    total_x = slab_rows * devices
    var_count = fields.shape[0]
    cells_y = fields.shape[2]
    cells_z = fields.shape[3]
    local_vars = jnp.einsum("vxyz,wxyz->vw", fields, fields, precision=highest)
    local_y = jnp.einsum("vxyz,vxuz->yu", fields, fields, precision=highest)
    flat = fields.reshape(-1, cells_z)
    local_z = jnp.dot(flat.T, flat, precision=highest, preferred_element_type=jnp.float32)
    summed_vars, summed_y, summed_z = lax.psum((local_vars, local_y, local_z), "gx")
    gram_vars = summed_vars / float(total_x * cells_y * cells_z)
    gram_y = summed_y / float(var_count * total_x * cells_z)
    gram_z = summed_z / float(var_count * total_x * cells_y)
    reduced_var = jnp.einsum("va,vxyz->axyz", factor_var, fields, precision=highest)
    reduced_z = jnp.einsum("axyz,zk->axyk", reduced_var, factor_z, precision=highest)
    reduced_y = jnp.einsum("axyk,yj->xajk", reduced_z, factor_y, precision=highest)
    comp_count = reduced_y.shape[1]
    projected = reduced_y.reshape(slab_rows, comp_count, reduced_y.shape[2] * reduced_y.shape[3])
    core_tensor = jnp.einsum(
        "xak,xr->kar",
        lax.all_to_all(projected, "gx", split_axis=2, concat_axis=0, tiled=True),
        factor_x,
        precision=highest,
    )
    return (core_tensor, gram_vars, gram_y, gram_z)


N = 16
V = 16
A = 8
S = 2
C = 256
R = 96
KP = 128
JD = R // N
CH = JD * S * A
GROUP = 4
TAIL = 24
PK = CH - TAIL
PIECE = 48


def split(value):
    high = value.astype(BF16)
    return high, (value - high.astype(F32)).astype(BF16)


def dot(a, b):
    return jnp.dot(a, b, preferred_element_type=F32)


def kernel(f_hbm, fy_ref, fz_ref, fv_ref, r_ref, gv_out, out,
           f_ref, h_ref, l_ref, zhl, yhl, pad, w_ref, p_ref, pk_ref, gy_acc, gz_acc, gv_acc,
           gram, recv_a, send_b, recv_b, send_c, recv_c, gv_all,
           s_load, s_core, r_core, s_gv, r_gv, s_a, r_a, s_b, r_b, s_c, r_c,
           s_cg, r_cg, s_bg, r_bg, s_ag, r_ag):
    me = lax.axis_index("gx")

    def load(i):
        x = i // (V // GROUP)
        first = lax.rem(i, V // GROUP) * GROUP
        part = pl.ds(first, GROUP)
        return pltpu.make_async_copy(f_hbm.at[part, x], f_ref.at[part, x], s_load.at[i])

    for i in range(S * V // GROUP):
        load(i).start()

    barrier = pltpu.get_barrier_semaphore()
    for off in range(1, N):
        pl.semaphore_signal(barrier, inc=1, device_id={"gx": lax.rem(me + off, N)}, device_id_type=MESH)

    def remote(src, dst, ssem, rsem, peer):
        return pltpu.make_async_remote_copy(
            src_ref=src, dst_ref=dst, send_sem=ssem, recv_sem=rsem,
            device_id={"gx": peer}, device_id_type=MESH)

    pad[...] = jnp.zeros((KP, C), F32)
    pad[0:R, :] = fz_ref[...]
    z_high, z_low = split(pad[...].T)
    zhl[:, 0:KP] = z_high
    zhl[:, KP:2 * KP] = z_low
    y_high, y_low = split(fy_ref[...])
    yhl[0:R, :] = y_high
    yhl[R:2 * R, :] = y_low

    def project(i, carry):
        x = i // (V // GROUP)
        first = lax.rem(i, V // GROUP) * GROUP
        for u in range(GROUP):
            v = first + u
            high, low = h_ref[v, x], l_ref[v, x]
            o = dot(yhl[...], jnp.concatenate([high, low], axis=1))
            along_y = o[0:R, 0:C] + (o[0:R, C:] + o[R:, 0:C])
            u_high, u_low = split(along_y)
            q = dot(jnp.concatenate([u_high, u_low], axis=0), zhl[...])
            w_ref[x * V + v] = q[0:R, 0:KP] + (q[0:R, KP:] + q[R:, 0:KP])
        return carry

    pl.semaphore_wait(barrier, N - 1)

    q4 = lax.rem(me, 4)
    core = lax.rem(me, 2)
    xx = lax.rem(me // 2, 2)
    zz = me // 4
    pair = me + 1 - 2 * core
    xpair = me + 2 - 4 * xx

    def zpeer(off):
        return lax.rem(zz + off, 4)

    def chunk(index):
        return pl.ds(pl.multiple_of(index * PK, 8), PK)

    def core_copy(dz, dq):
        peer = zpeer(dz) * 4 + lax.rem(q4 + dq, 4)
        sem = dz * 4 + dq
        return remote(pk_ref.at[chunk(peer)], r_ref.at[chunk(me)], s_core.at[sem], r_core.at[sem], peer)

    gy_acc[...] = jnp.zeros((2 * C, C), F32)
    gz_acc[...] = jnp.zeros((C, 2 * C), F32)
    gv_acc[...] = jnp.zeros((2 * C, C), F32)

    def grams(i, carry):
        x = i // (V // GROUP)
        first = lax.rem(i, V // GROUP) * GROUP
        load(i).wait()
        parts = [split(f_ref[first + u, x]) for u in range(GROUP)]
        highs = [high for high, low in parts]
        lows = [low for high, low in parts]
        for u in range(GROUP):
            h_ref[first + u, x] = highs[u]
            l_ref[first + u, x] = lows[u]
        turned = [h.T for h in highs]
        both = jnp.concatenate([jnp.concatenate(highs, axis=1), jnp.concatenate(lows, axis=1)], axis=0)
        gy_acc[...] += dot(both, jnp.concatenate(turned, axis=0))
        wide = jnp.concatenate([jnp.concatenate(highs, axis=0), jnp.concatenate(lows, axis=0)], axis=1)
        gz_acc[...] += dot(jnp.concatenate(turned, axis=1), wide)
        return carry

    lax.fori_loop(0, S * V // GROUP, grams, 0)

    def gram_v(i, carry):
        x = i // (V // GROUP)
        first = lax.rem(i, V // GROUP) * GROUP
        rows = [pl.ds(pl.multiple_of((first + u) * 16, 16), 16) for u in range(GROUP)]
        vh = jnp.concatenate([h_ref[:, x, r, :].reshape(C, C) for r in rows], axis=1)
        vl = jnp.concatenate([l_ref[:, x, r, :].reshape(C, C) for r in rows], axis=1)
        gv_acc[...] += lax.dot_general(
            jnp.concatenate([vh, vl], axis=0), vh, (((1,), (1,)), ((), ())), preferred_element_type=F32)
        return carry

    whole_y = gy_acc[0:C, :] + (gy_acc[C:, :] + gy_acc[C:, :].T)
    whole_z = gz_acc[:, 0:C] + (gz_acc[:, C:] + gz_acc[:, C:].T)
    for m, whole in enumerate((whole_y, whole_z)):
        gram[m * 384:m * 384 + 128, :] = whole[0:128, 0:128]
        gram[m * 384 + 128:m * 384 + 256, :] = whole[0:128, 128:]
        gram[m * 384 + 256:m * 384 + 384, :] = whole[128:, 128:]

    def piece(c, x, z):
        return pl.ds(pl.multiple_of(((c * 2 + x) * 4 + z) * PIECE, 8), PIECE)

    order = (1, 2, 3, 0)

    def a_copy(k, off):
        x = (1 - xx) if k == 0 else xx
        sem = k * 4 + off
        return remote(gram.at[piece(1 - core, x, zpeer(off))], recv_a.at[sem], s_a.at[sem], r_a.at[sem], pair)

    for k in range(2):
        for off in order:
            a_copy(k, off).start()

    lax.fori_loop(0, V // GROUP, project, 0)

    def gv_copy(off):
        return remote(gv_all.at[me], gv_all.at[me], s_gv.at[off], r_gv.at[off], lax.rem(me + off, N))

    def b_copy(off):
        return remote(send_b.at[off], recv_b.at[off], s_b.at[off], r_b.at[off], xpair)

    def c_copy(off):
        return remote(send_c.at[off], recv_c.at[off], s_c.at[off], r_c.at[off], zpeer(off) * 4 + q4)

    for off in order:
        a_copy(0, off).wait()
        send_b[off] = gram[piece(core, 1 - xx, zpeer(off)), :] + recv_a[off]
        b_copy(off).start()

    lax.fori_loop(V // GROUP, S * V // GROUP, project, 0)

    for x in range(S):
        for a in range(A):
            total = fv_ref[a, 0] * w_ref[x * V]
            for v in range(1, V):
                total = total + fv_ref[a, v] * w_ref[x * V + v]
            p_ref[pl.ds(x * A + a, R, stride=S * A), :] = total

    lane = lax.broadcasted_iota(jnp.int32, (TAIL, KP), 1)
    for d in range(N):
        tail = p_ref[d * CH + PK:(d + 1) * CH, :]
        for t in range(3):
            rolled = pltpu.roll(tail, R - 32 * t, 1)
            pk_ref[d * PK + t * TAIL:d * PK + (t + 1) * TAIL, :] = jnp.where(
                lane >= R, rolled, p_ref[d * CH + t * TAIL:d * CH + (t + 1) * TAIL, :])

    for off in order:
        a_copy(1, off).wait()
        partial = gram[piece(core, xx, zpeer(off)), :] + recv_a[4 + off]
        b_copy(off).wait()
        send_c[off] = partial + recv_b[off]
        if off:
            c_copy(off).start()

    others = [(dz, dq) for dz in (2, 1, 3, 0) for dq in range(4) if dz or dq]
    for dz, dq in others:
        core_copy(dz, dq).start()
    r_ref[chunk(me), :] = pk_ref[chunk(me), :]

    lax.fori_loop(0, S * V // GROUP, gram_v, 0)
    row = lax.broadcasted_iota(jnp.int32, (C, C), 0)
    col = lax.broadcasted_iota(jnp.int32, (C, C), 1)
    whole = gv_acc[0:C, :] + (gv_acc[C:, :] + gv_acc[C:, :].T)
    kept = jnp.where(lax.rem(row, 16) == lax.rem(col, 16), whole, 0.0)
    pick_col = (lax.broadcasted_iota(jnp.int32, (C, KP), 0) // 16
                == lax.broadcasted_iota(jnp.int32, (C, KP), 1)).astype(F32)
    pick_row = (lax.broadcasted_iota(jnp.int32, (V, C), 1) // 16
                == lax.broadcasted_iota(jnp.int32, (V, C), 0)).astype(F32)
    highest = lax.Precision.HIGHEST
    by_col = jnp.dot(kept, pick_col, precision=highest, preferred_element_type=F32)
    by_both = jnp.dot(pick_row, by_col, precision=highest, preferred_element_type=F32)
    gv_all[me] = by_both[0:8, :] + pltpu.roll(by_both[8:16, :], 16, 1)

    for off in range(1, N):
        gv_copy(off).start()
    mine = send_c[0]
    for off in range(1, 4):
        c_copy(off).wait()
        mine = mine + recv_c[off]
    out[piece(core, xx, zz), :] = mine * (1.0 / float(V * S * N * C))

    def cg_copy(off):
        at = piece(core, xx, zz)
        return remote(out.at[at], out.at[at], s_cg.at[off], r_cg.at[off], zpeer(off) * 4 + q4)

    def bg_copy(off):
        at = piece(core, xx, zpeer(4 - off))
        return remote(out.at[at], out.at[at], s_bg.at[off], r_bg.at[off], xpair)

    def ag_copy(k, off):
        at = piece(core, xx if k == 0 else 1 - xx, zpeer(4 - off))
        sem = k * 4 + off
        return remote(out.at[at], out.at[at], s_ag.at[sem], r_ag.at[sem], pair)

    for off in range(1, 4):
        cg_copy(off).start()
    for off in range(4):
        if off:
            cg_copy(off).wait()
        bg_copy(off).start()
        ag_copy(0, off).start()
    for off in range(4):
        bg_copy(off).wait()
        ag_copy(1, off).start()

    for off in range(1, N):
        gv_copy(off).wait()
    total = gv_all[0]
    for d in range(1, N):
        total = total + gv_all[d]
    gv_out[...] = total
    for dz, dq in others:
        core_copy(dz, dq).wait()
    for k in range(2):
        for off in range(4):
            ag_copy(k, off).wait()


def finish(r_hbm, fx_ref, gram_hbm, gv_hbm, core_hbm, gv_out, gy_out, gz_out,
           r_ref, gram_ref, gv_ref, un_ref, core_ref, s_in, sems):
    loads = [pltpu.make_async_copy(src, dst, s_in.at[i]) for i, (src, dst) in enumerate(
        ((r_hbm, r_ref), (gram_hbm, gram_ref), (gv_hbm, gv_ref)))]
    for load in loads:
        load.start()
    loads[0].wait()

    lane = lax.broadcasted_iota(jnp.int32, (TAIL, KP), 1)
    for d in range(N):
        parts = [r_ref[d * PK + t * TAIL:d * PK + (t + 1) * TAIL, :] for t in range(3)]
        for t in range(3):
            un_ref[d * CH + t * TAIL:d * CH + (t + 1) * TAIL, :] = parts[t]
        rolled = [pltpu.roll(parts[t], 32 * (t + 1), 1) for t in range(3)]
        un_ref[d * CH + PK:(d + 1) * CH, :] = jnp.where(
            lane < 32, rolled[0], jnp.where(lane < 64, rolled[1], rolled[2]))

    fx_high, fx_low = split(jnp.concatenate(
        [fx_ref[pl.ds(x, N, stride=S), :] for x in range(S)], axis=0))
    weights = jnp.concatenate([fx_high, fx_high, fx_low], axis=0).T
    copies = []
    for a in range(A):
        slabs = [jnp.concatenate(
            [un_ref[pl.ds(j * S * A + x * A + a, N, stride=CH), 0:R] for x in range(S)], axis=0)
            for j in range(JD)]
        high, low = split(jnp.concatenate(slabs, axis=1))
        core_ref[a] = dot(weights, jnp.concatenate([high, low, high], axis=0))
        copy = pltpu.make_async_copy(core_ref.at[a], core_hbm.at[a], sems.at[a])
        copy.start()
        copies.append(copy)

    loads[1].wait()
    loads[2].wait()
    scale = 1.0 / float(S * N * C * C)
    gv_out[0:8, :] = gv_ref[:, 0:V] * scale
    gv_out[8:16, :] = gv_ref[:, V:2 * V] * scale
    for m, o_ref in enumerate((gy_out, gz_out)):
        o_ref[0:128, 0:128] = gram_ref[m * 384:m * 384 + 128, :]
        off_block = gram_ref[m * 384 + 128:m * 384 + 256, :]
        o_ref[0:128, 128:] = off_block
        o_ref[128:, 0:128] = off_block.T
        o_ref[128:, 128:] = gram_ref[m * 384 + 256:m * 384 + 384, :]
    for copy in copies:
        copy.wait()


def fused(fields, factor_x, factor_y, factor_z, factor_var):
    vmem = pl.BlockSpec(memory_space=pltpu.VMEM)
    anywhere = pl.BlockSpec(memory_space=pl.ANY)
    in_hbm = pl.BlockSpec(memory_space=pltpu.HBM)
    dma = pltpu.SemaphoreType.DMA
    received, gv, gram = pl.pallas_call(
        kernel,
        out_shape=(
            jax.ShapeDtypeStruct((N * PK, KP), F32),
            jax.ShapeDtypeStruct((8, KP), F32),
            jax.ShapeDtypeStruct((16 * PIECE, 128), F32),
        ),
        in_specs=[anywhere, vmem, vmem, pl.BlockSpec(memory_space=pltpu.SMEM)],
        out_specs=(vmem, vmem, vmem),
        scratch_shapes=[
            pltpu.VMEM((V, S, C, C), F32),
            pltpu.VMEM((V, S, C, C), BF16), pltpu.VMEM((V, S, C, C), BF16),
            pltpu.VMEM((C, 2 * KP), BF16), pltpu.VMEM((2 * R, C), BF16), pltpu.VMEM((KP, C), F32),
            pltpu.VMEM((S * V, R, KP), F32),
            pltpu.VMEM((R * S * A, KP), F32), pltpu.VMEM((N * PK, KP), F32),
            pltpu.VMEM((2 * C, C), F32), pltpu.VMEM((C, 2 * C), F32), pltpu.VMEM((2 * C, C), F32),
            pltpu.VMEM((16 * PIECE, 128), F32), pltpu.VMEM((8, PIECE, 128), F32),
            pltpu.VMEM((4, PIECE, 128), F32), pltpu.VMEM((4, PIECE, 128), F32),
            pltpu.VMEM((4, PIECE, 128), F32), pltpu.VMEM((4, PIECE, 128), F32),
            pltpu.VMEM((N, 8, KP), F32),
            dma((S * V // GROUP,)), dma((N,)), dma((N,)), dma((N,)), dma((N,)),
            dma((8,)), dma((8,)), dma((4,)), dma((4,)), dma((4,)), dma((4,)),
            dma((4,)), dma((4,)), dma((4,)), dma((4,)), dma((8,)), dma((8,)),
        ],
        compiler_params=pltpu.CompilerParams(
            collective_id=0, has_side_effects=True, vmem_limit_bytes=56 * 1024 * 1024),
        name="fused",
    )(fields, factor_y.T, factor_z.T, factor_var.T)
    core, gram_v, gram_y, gram_z = pl.pallas_call(
        finish,
        out_shape=(
            jax.ShapeDtypeStruct((A, R, JD * R), F32),
            jax.ShapeDtypeStruct((V, V), F32),
            jax.ShapeDtypeStruct((C, C), F32),
            jax.ShapeDtypeStruct((C, C), F32),
        ),
        in_specs=[in_hbm, vmem, in_hbm, in_hbm],
        out_specs=(anywhere, vmem, vmem, vmem),
        scratch_shapes=[
            pltpu.VMEM((N * PK, KP), F32), pltpu.VMEM((16 * PIECE, 128), F32), pltpu.VMEM((8, KP), F32),
            pltpu.VMEM((N * CH, KP), F32), pltpu.VMEM((A, R, JD * R), F32), dma((3,)), dma((A,))],
        compiler_params=pltpu.CompilerParams(vmem_limit_bytes=60 * 1024 * 1024),
        name="finish",
    )(received, factor_x, gram, gv)
    return core.transpose(2, 0, 1), gram_v, gram_y, gram_z


def local(fields, factor_x, factor_y, factor_z, factor_var):
    sizes = (fields.shape, factor_x.shape, factor_y.shape, factor_z.shape, factor_var.shape)
    served = ((V, S, C, C), (S * N, R), (C, R), (C, R), (V, A))
    if lax.axis_size("gx") == N and sizes == served:
        return fused(fields, factor_x, factor_y, factor_z, factor_var)
    return plain(fields, factor_x, factor_y, factor_z, factor_var)


def solution(mesh):
    in_specs = (
        P("grp", "gx", None, None),
        P("grp", None),
        P("grp", None),
        P("grp", None),
        P("grp", None),
    )
    out_specs = (P(("grp", "gx"), None, None), P("grp", None), P("grp", None), P("grp", None))
    return jax.shard_map(local, mesh=mesh, in_specs=in_specs, out_specs=out_specs, check_vma=False)
```
